32 devices in a mesh: face: 4 (over y, x), col: 8 (over z, core).
Axes of the slice: x: 2, y: 2, z: 4, core: 2. Of those that a mesh axis runs over, the one named last changes fastest.
Arguments:
- dyn_state: float32 [16, 64, 16, 720], P('face', 'col'), may hold values from -6 to 6
- edge_links: int32 [16, 64, 4], P('face', 'col'), may hold values from 0 to 8191, as said below
- phys_slot: int32 [16, 64, 4], P('face', 'col'), may hold values from 0 to 4095, as said below
- crm_active: int32 [4096], P(('face', 'col')), may hold values 0 or 1
- crm_state: bfloat16 [10, 32, 64, 4096], P(None, None, None, ('face', 'col')), may hold values from -4 to 4
Outputs:
- dyn_new: float32 [16, 64, 16, 720], P('face', 'col')
- column_tend: float32 [16, 64, 4, 320], P('face', 'col')
- crm_new: bfloat16 [10, 32, 64, 4096], P(None, None, None, ('face', 'col'))
The draws below stay inside these ranges and needn't reach their ends.
Inputs may be any that keep to these rules, and one draw needn't show every extreme that they name: `edge_links`: each entry is 8 n + 2 k' + r: element n (id row * 64 + column in a grid of 16 x 64 elements), its edge k' (0 to 3) and a reversal bit r. For edge 0 of element (row, column) n lies in row - 1, for edge 2 in row + 1, for edge 1 in column + 1, for edge 3 in column - 1, rows modulo 16 and columns modulo 64; the other coordinate differs by at most one. `phys_slot`: A permutation of the physics columns. The physics column p lives on device p // 128 of face+col; of the quadrants on one device of the element layout exactly 4 go to each device.
All inputs are finite; a program needn't handle non-finite values. No bound on the sum of `crm_active` on one device may be relied on, other than what follows from the above.
Results may differ from the reference program's by a relative error of at most 0.001.
Values sent between devices are 32-bit elements; how exact they have to be, the bound alone decides.
A program may use at most 192 MiB of HBM per device.

```python
import jax
import jax.numpy as jnp
import numpy as np
from jax import lax

NP = 4
NFLD = 10
LEV = 72
CLEV = 32
CX = 64
DSTEPS = 2
CSTEPS = 2
ER = 4
EC = 8
NR = 16
NC = 64
COLS_DEV = 128
COLS = 4096


def draw_edge_links(key, part):
    keys = jax.random.split(jax.random.fold_in(key, 11), 3)
    shape = (NR, NC, 4)
    offset = jax.random.randint(keys[0], shape, -1, 2)
    other = jax.random.randint(keys[1], shape, 0, 4)
    reversal = jax.random.randint(keys[2], shape, 0, 2)
    rows = lax.broadcasted_iota(jnp.int32, shape, 0)
    cols = lax.broadcasted_iota(jnp.int32, shape, 1)
    edge = lax.broadcasted_iota(jnp.int32, shape, 2)
    top_end = (rows == 0) & (cols == NC - 1) & (edge == 0)
    low_end = (rows == 1) & (cols == 0) & (edge == 0)
    offset = jnp.where(top_end | low_end, 0, offset)
    other = jnp.where(top_end, 3, jnp.where(low_end, 0, other))
    reversal = jnp.where(top_end, 1, jnp.where(low_end, 0, reversal))
    drow = jnp.where(edge == 0, -1, jnp.where(edge == 2, 1, offset))
    dcol = jnp.where(edge == 1, 1, jnp.where(edge == 3, -1, offset))
    near_row = (rows + drow) % NR
    near_col = (cols + dcol) % NC
    return ((near_row * NC + near_col) * 8 + other * 2 + reversal).astype(jnp.int32)


def draw_phys_slot(key, part):
    nface = NR // ER
    ncol = NC // EC
    ndev = nface * ncol
    per_dev = 4 * ER * EC
    count = per_dev // ndev
    first, second = jax.random.split(jax.random.fold_in(key, 23))
    ranks = jax.vmap(lambda sub: jax.random.permutation(sub, per_dev))(jax.random.split(first, ndev))
    places = jax.vmap(lambda sub: jax.random.permutation(sub, per_dev))(jax.random.split(second, ndev))
    target = ranks // count
    within = ranks % count
    source = jnp.arange(ndev, dtype=jnp.int32)[:, None]
    slot = places[target, source * count + within]
    global_slot = (target * per_dev + slot).astype(jnp.int32)
    laid = global_slot.reshape(nface, ncol, ER, EC, 4).transpose(0, 2, 1, 3, 4)
    return laid.reshape(NR, NC, 4)


def plant(values, own_key, least, top_value):
    longest = values.shape.index(max(values.shape))
    spots = []
    for shift in (0, 1):
        where = [jax.random.randint(jax.random.fold_in(own_key, axis), (), 0, length) for axis, length in enumerate(values.shape)]
        where[longest] = (where[longest] + shift) % values.shape[longest]
        spots.append(tuple(where))
    return values.at[spots[0]].set(least).at[spots[1]].set(top_value)


def levels(own_key, dims, shards, low, high):
    def one(axis_at, shards_of):
        heights = jax.random.uniform(jax.random.fold_in(jax.random.fold_in(own_key, 6), axis_at), (shards_of,), jnp.float32, low / len(shards), high / len(shards))
        return jnp.repeat(jnp.exp(heights), dims[axis_at] // shards_of).reshape((-1,) + (1,) * (len(dims) - axis_at - 1))

    level = one(*shards[0])
    for cut in shards[1:]:
        level = level * one(*cut)
    return level


def scatter_about(rng, dims, scale, bound, cuts=(), held_as=jnp.bfloat16):
    drawn = jax.random.normal(rng, dims, jnp.float32) * scale
    if len(cuts) > 0:
        drawn = levels(rng, dims, cuts, -0.22, 0.18) * drawn
    return jnp.clip(drawn, min=-bound, max=bound).astype(held_as)


def setup_inputs(seed: int = 0) -> dict:
    seeds = jax.random.split(jax.random.key(seed), 6)
    return {
        "dyn_state": scatter_about(seeds[0], (NR, NC, NP * NP, NFLD * LEV), 1.0, 6.0, ((0, 4), (1, 8)), jnp.float32),
        "edge_links": draw_edge_links(jax.random.fold_in(seeds[5], 71), 0),
        "phys_slot": draw_phys_slot(jax.random.fold_in(seeds[5], 71), 0),
        "crm_active": plant((jax.random.randint(seeds[3], (COLS,), 0, 4) < 3).astype(jnp.int32), jax.random.fold_in(seeds[3], 1), 0, 1),
        "crm_state": scatter_about(seeds[4], (NFLD, CLEV, CX, COLS), 1.0, 4.0, ((3, 32),)),
    }


KAPPA = 0.1
ADVECT = 0.1
DIFF_X = 0.2
DIFF_Z = 0.1
RELAX = 0.2
CONVERT = 0.5


def node_tables():
    laplace = np.zeros((16, 16), np.float32)
    for row_a in range(4):
        for row_b in range(4):
            here = row_a * 4 + row_b
            for step_a, step_b in ((1, 0), (-1, 0), (0, 1), (0, -1)):
                near_a, near_b = row_a + step_a, row_b + step_b
                if 0 <= near_a < 4 and 0 <= near_b < 4:
                    laplace[here, near_a * 4 + near_b] += 1.0
                    laplace[here, here] -= 1.0
    edge_nodes = np.array([[0, 1, 2, 3], [3, 7, 11, 15], [12, 13, 14, 15], [0, 4, 8, 12]])
    spread = np.zeros((16, 16), np.float32)
    for edge in range(4):
        for point in range(4):
            spread[edge_nodes[edge, point], edge * 4 + point] = 1.0
    denom = 1.0 + spread.sum(axis=1)
    quarter = np.zeros((4, 16), np.float32)
    for row_a in range(4):
        for row_b in range(4):
            quarter[(row_a // 2) * 2 + row_b // 2, row_a * 4 + row_b] = 0.25
    return laplace, spread, denom, quarter


def matched_points(links):
    other_edge = (links // 2) % 4
    reversal = links % 2
    points = jnp.arange(4, dtype=jnp.int32)
    along = jnp.where(reversal[..., None] == 1, 3 - points, points)
    base = jnp.where(other_edge == 1, 3, jnp.where(other_edge == 2, 12, 0))
    stride = jnp.where((other_edge == 1) | (other_edge == 3), 4, 1)
    return (base[..., None] + stride[..., None] * along).astype(jnp.int32)


def crm_run(state, forcing, active):
    start_mean = jnp.mean(state, axis=2)
    live = (active == 1)[None, None, None, :]
    for step in range(CSTEPS):
        east = jnp.roll(state, -1, axis=2)
        west = jnp.roll(state, 1, axis=2)
        upper = jnp.concatenate([state[:, 1:], state[:, -1:]], axis=1)
        lower = jnp.concatenate([state[:, :1], state[:, :-1]], axis=1)
        mean_x = jnp.mean(state, axis=2, keepdims=True)
        fresh = (state - ADVECT * state[0:1] * (east - west) + DIFF_X * (east + west - 2.0 * state)
                 + DIFF_Z * (upper + lower - 2.0 * state) + RELAX * (forcing[:, :, None, :] - mean_x))
        cond = CONVERT * jnp.maximum(fresh[3:4] - fresh[2:3], 0.0)
        fresh = jnp.concatenate([fresh[:3], fresh[3:4] - cond, fresh[4:5] + cond, fresh[5:]], axis=0)
        state = jnp.where(live, fresh, state)
    tend = (jnp.mean(state, axis=2) - start_mean) / CSTEPS
    return state, tend


def reference(dyn_state, edge_links, phys_slot, crm_active, crm_state):
    laplace, spread, denom, quarter = [jnp.asarray(table) for table in node_tables()]
    width = NFLD * LEV
    elems = NR * NC
    state = dyn_state.reshape(elems, 16, width)
    links = edge_links.reshape(elems, 4)
    neighbour = links // 8
    pick = matched_points(links)
    index_flat = (neighbour[..., None] * 16 + pick).reshape(-1)
    for step in range(DSTEPS):
        state = state + KAPPA * jnp.einsum("nm,emw->enw", laplace, state, precision=lax.Precision.HIGHEST)
        matched = state.reshape(elems * 16, width)[index_flat].reshape(elems, 16, width)
        summed = jnp.einsum("nm,emw->enw", spread, matched, precision=lax.Precision.HIGHEST)
        state = (state + summed) / denom[None, :, None]
    dyn_new = state.reshape(NR, NC, 16, width)
    columns = jnp.einsum("qn,enw->eqw", quarter, state, precision=lax.Precision.HIGHEST).reshape(COLS, width)
    slots = phys_slot.reshape(-1)
    physics = jnp.zeros((COLS, width), jnp.float32).at[slots].set(columns)
    forcing = physics.reshape(COLS, NFLD, LEV)[:, :, :CLEV].transpose(1, 2, 0)
    blocks = COLS // COLS_DEV
    blocked_state = crm_state.astype(jnp.float32).reshape(NFLD, CLEV, CX, blocks, COLS_DEV).transpose(3, 0, 1, 2, 4)
    blocked_force = forcing.reshape(NFLD, CLEV, blocks, COLS_DEV).transpose(2, 0, 1, 3)
    blocked_live = crm_active.reshape(blocks, COLS_DEV)

    def one_block(items):
        final, tend = crm_run(items[0], items[1], items[2])
        return final.astype(jnp.bfloat16), tend

    finals, tends = lax.map(one_block, (blocked_state, blocked_force, blocked_live))
    crm_new = finals.transpose(1, 2, 3, 0, 4).reshape(NFLD, CLEV, CX, COLS)
    tend_all = tends.transpose(1, 2, 0, 3).reshape(NFLD * CLEV, COLS)
    column_tend = tend_all.T[slots].reshape(NR, NC, 4, NFLD * CLEV)
    return dyn_new, column_tend, crm_new
```

```python
import jax
import jax.numpy as jnp
import numpy as np
from jax import lax
from jax.experimental import pallas as pl
from jax.experimental.pallas import tpu as pltpu
from jax.sharding import PartitionSpec as P

NFLD = 10
LEV = 72
CLEV = 32
DSTEPS = 2
CSTEPS = 2


KAPPA = 0.1
ADVECT = 0.1
DIFF_X = 0.2
DIFF_Z = 0.1
RELAX = 0.2
CONVERT = 0.5


def extended_2(cells, sides, width):
    for axis, dim in sides:
        count = lax.axis_size(axis)
        head = lax.slice_in_dim(cells, 0, width, axis=dim)
        tail = lax.slice_in_dim(cells, cells.shape[dim] - width, cells.shape[dim], axis=dim)
        cells = jnp.concatenate(
            [
                lax.ppermute(tail, axis, [(i, (i + 1) % count) for i in range(count)]),
                cells,
                lax.ppermute(head, axis, [((i + 1) % count, i) for i in range(count)]),
            ],
            axis=dim,
        )
    return cells


def node_tables():
    laplace = np.zeros((16, 16), np.float32)
    for row_a in range(4):
        for row_b in range(4):
            here = row_a * 4 + row_b
            for step_a, step_b in ((1, 0), (-1, 0), (0, 1), (0, -1)):
                near_a, near_b = (row_a + step_a, row_b + step_b)
                if 0 <= near_a < 4 and 0 <= near_b < 4:
                    laplace[here, near_a * 4 + near_b] += 1.0
                    laplace[here, here] -= 1.0
    edge_nodes = np.array([[0, 1, 2, 3], [3, 7, 11, 15], [12, 13, 14, 15], [0, 4, 8, 12]])
    spread = np.zeros((16, 16), np.float32)
    for edge in range(4):
        for point in range(4):
            spread[edge_nodes[edge, point], edge * 4 + point] = 1.0
    denom = 1.0 + spread.sum(axis=1)
    quarter = np.zeros((4, 16), np.float32)
    for row_a in range(4):
        for row_b in range(4):
            quarter[row_a // 2 * 2 + row_b // 2, row_a * 4 + row_b] = 0.25
    return (laplace, spread, denom, quarter)


def matched_points(links):
    other_edge = links // 2 % 4
    reversal = links % 2
    points = jnp.arange(4, dtype=jnp.int32)
    along = jnp.where(reversal[..., None] == 1, 3 - points, points)
    base = jnp.where(other_edge == 1, 3, jnp.where(other_edge == 2, 12, 0))
    stride = jnp.where((other_edge == 1) | (other_edge == 3), 4, 1)
    return base[..., None] + stride[..., None] * along


def crm_kernel(force_ref, active_ref, state_hbm, out_hbm, tend_ref, held, first, final, begin, in_sem, out_sem):
    nfld, clev, cx, cols = held.shape
    part = clev // 4

    def fetch(i):
        return pltpu.make_async_copy(
            state_hbm.at[:, pl.ds(i * part, part)], held.at[:, pl.ds(i * part, part)], in_sem.at[i]
        )

    def emit(i):
        return pltpu.make_async_copy(
            final.at[:, pl.ds(i * part, part)], out_hbm.at[:, pl.ds(i * part, part)], out_sem.at[i]
        )

    for i in range(4):
        fetch(i).start()
    live = jnp.broadcast_to(active_ref[...] == 1, (cx, cols))

    def advance(src, z, store):
        above = jnp.minimum(z + 1, clev - 1)
        below = jnp.maximum(z - 1, 0)
        wind = ADVECT * src[0, z].astype(jnp.float32)
        from_east = DIFF_X - wind
        from_west = DIFF_X + wind

        def one(f):
            q = src[f, z].astype(jnp.float32)
            mean = jnp.sum(q, axis=0, keepdims=True) * (1.0 / cx)
            push = RELAX * (force_ref[f, pl.ds(z, 1), :] - mean)
            near = src[f, above].astype(jnp.float32) + src[f, below].astype(jnp.float32)
            fresh = (
                (1.0 - 2.0 * DIFF_X - 2.0 * DIFF_Z) * q
                + from_east * pltpu.roll(q, cx - 1, 0)
                + from_west * pltpu.roll(q, 1, 0)
                + DIFF_Z * near
                + push
            )
            return q, fresh, mean

        for f in range(nfld):
            q, fresh, mean = one(f)
            if f == 2:
                second = fresh
            if f == 3:
                cond = CONVERT * jnp.maximum(fresh - second, 0.0)
                fresh = fresh - cond
            if f == 4:
                fresh = fresh + cond
            store(f, z, jnp.where(live, fresh, q), mean)

    def store_first(f, z, value, mean):
        first[f, z] = value
        begin[f, pl.ds(z, 1), :] = mean

    def store_final(f, z, value, mean):
        final[f, z] = value.astype(final.dtype)
        end = jnp.sum(value, axis=0, keepdims=True) * (1.0 / cx)
        tend_ref[f, pl.ds(z, 1), :] = (end - begin[f, pl.ds(z, 1), :]) * (1.0 / CSTEPS)

    fetch(0).wait()
    fetch(1).wait()
    advance(held, 0, store_first)
    for i in range(4):
        if 1 <= i < 3:
            fetch(i + 1).wait()

        @pl.loop(max(1, i * part), (i + 1) * part)
        def _(z):
            advance(held, z, store_first)
            advance(first, z - 1, store_final)

        if i >= 1:
            emit(i - 1).start()
    advance(first, clev - 1, store_final)
    emit(3).start()
    for i in range(4):
        emit(i).wait()


def crm_run(state, forcing, active):
    nfld, clev, cx, cols = state.shape
    vmem = pl.BlockSpec(memory_space=pltpu.VMEM)
    hbm = pl.BlockSpec(memory_space=pl.ANY)
    return pl.pallas_call(
        crm_kernel,
        out_shape=(
            jax.ShapeDtypeStruct(state.shape, state.dtype),
            jax.ShapeDtypeStruct((nfld, clev, cols), jnp.float32),
        ),
        in_specs=[vmem, vmem, hbm],
        out_specs=(hbm, vmem),
        scratch_shapes=[
            pltpu.VMEM(state.shape, state.dtype),
            pltpu.VMEM(state.shape, jnp.float32),
            pltpu.VMEM(state.shape, state.dtype),
            pltpu.VMEM((nfld, clev, cols), jnp.float32),
            pltpu.SemaphoreType.DMA((4,)),
            pltpu.SemaphoreType.DMA((4,)),
        ],
        compiler_params=pltpu.CompilerParams(vmem_limit_bytes=36 * 2**20),
    )(forcing, active.reshape(1, cols), state)


def per_device(dyn_state, edge_links, phys_slot, crm_active, crm_state):
    exact = lax.Precision.HIGHEST
    laplace, spread, denom, quarter = [jnp.asarray(table) for table in node_tables()]
    rows_dev, cols_dev, nodes, width = dyn_state.shape
    nface = lax.axis_size("face")
    ncol = lax.axis_size("col")
    ndev = nface * ncol
    total_rows = rows_dev * nface
    total_cols = cols_dev * ncol
    neighbour = edge_links // 8
    pick = matched_points(edge_links)
    near_row = neighbour // total_cols
    near_col = neighbour % total_cols
    local_row = lax.broadcasted_iota(jnp.int32, (rows_dev, cols_dev, 4), 0)
    local_col = lax.broadcasted_iota(jnp.int32, (rows_dev, cols_dev, 4), 1)
    drow = (near_row - (lax.axis_index("face") * rows_dev + local_row) + 1) % total_rows - 1
    dcol = (near_col - (lax.axis_index("col") * cols_dev + local_col) + 1) % total_cols - 1
    place = (local_row + drow + 1) * (cols_dev + 2) + (local_col + dcol + 1)
    index_flat = place[..., None] * 16 + pick
    index_flat = index_flat.reshape(-1)
    state = dyn_state
    for step in range(DSTEPS):
        state = state + KAPPA * jnp.einsum(
            "nm,rcmw->rcnw", laplace, state, precision=lax.Precision.HIGHEST
        )
        extended = extended_2(state, (("face", 0), ("col", 1)), 1)
        matched = jnp.take(extended.reshape(-1, width), index_flat, axis=0).reshape(
            rows_dev, cols_dev, 16, width
        )
        summed = jnp.einsum("nm,rcmw->rcnw", spread, matched, precision=lax.Precision.HIGHEST)
        state = (state + summed) / denom[None, None, :, None]
    columns = jnp.einsum("qn,rcnw->rcqw", quarter, state, precision=exact).reshape(-1, width)
    per_dev = columns.shape[0]
    count = per_dev // ndev
    depth = NFLD * CLEV
    wanted = (np.arange(NFLD)[:, None] * LEV + np.arange(CLEV)).reshape(-1)
    keep = jnp.asarray(np.arange(width)[:, None] == wanted[None, :], jnp.float32)
    keys_local = phys_slot.reshape(-1)
    rank = jnp.sum((keys_local[None, :] < keys_local[:, None]).astype(jnp.int32), axis=1)
    sorting = rank[None, :] == jnp.arange(per_dev, dtype=jnp.int32)[:, None]
    out_keys = jnp.sum(jnp.where(sorting, keys_local[None, :], 0), axis=1)
    arrived_keys = lax.all_to_all(
        out_keys.reshape(ndev, count), ("face", "col"), split_axis=0, concat_axis=0, tiled=True
    )
    slots = arrived_keys.reshape(-1) % per_dev
    landing = (slots[:, None] == jnp.arange(per_dev, dtype=jnp.int32)[None, :]).astype(jnp.float32)
    sorting = sorting.astype(jnp.float32)
    outgoing = jnp.dot(sorting, jnp.dot(columns, keep, precision=exact), precision=exact)
    arrived = lax.all_to_all(
        outgoing.reshape(ndev, count, depth),
        ("face", "col"),
        split_axis=0,
        concat_axis=0,
        tiled=True,
    )
    forcing = jnp.einsum("sw,sc->wc", arrived.reshape(per_dev, depth), landing, precision=exact)
    crm_new, tend = crm_run(crm_state, forcing.reshape(NFLD, CLEV, per_dev), crm_active)
    tend_rows = jnp.einsum("sc,wc->sw", landing, tend.reshape(depth, per_dev), precision=exact)
    returned = lax.all_to_all(
        tend_rows.reshape(ndev, count, depth),
        ("face", "col"),
        split_axis=0,
        concat_axis=0,
        tiled=True,
    )
    placed = jnp.einsum("pi,pw->iw", sorting, returned.reshape(per_dev, depth), precision=exact)
    column_tend = placed.reshape(rows_dev, cols_dev, 4, depth)
    return (state, column_tend, crm_new)


def solution(mesh):
    return jax.shard_map(
        per_device,
        mesh=mesh,
        in_specs=(
            P("face", "col", None, None),
            P("face", "col", None),
            P("face", "col", None),
            P(("face", "col")),
            P(None, None, None, ("face", "col")),
        ),
        out_specs=(
            P("face", "col", None, None),
            P("face", "col", None, None),
            P(None, None, None, ("face", "col")),
        ),
        check_vma=False,
    )
```

```python
import functools

import jax
import jax.numpy as jnp
import numpy as np
from jax import lax
from jax.experimental import pallas as pl
from jax.experimental.pallas import tpu as pltpu
from jax.sharding import PartitionSpec as P

NFLD = 10
LEV = 72
CLEV = 32
DSTEPS = 2
CSTEPS = 2


KAPPA = 0.1
ADVECT = 0.1
DIFF_X = 0.2
DIFF_Z = 0.1
RELAX = 0.2
CONVERT = 0.5


def node_tables():
    laplace = np.zeros((16, 16), np.float32)
    for row_a in range(4):
        for row_b in range(4):
            here = row_a * 4 + row_b
            for step_a, step_b in ((1, 0), (-1, 0), (0, 1), (0, -1)):
                near_a, near_b = (row_a + step_a, row_b + step_b)
                if 0 <= near_a < 4 and 0 <= near_b < 4:
                    laplace[here, near_a * 4 + near_b] += 1.0
                    laplace[here, here] -= 1.0
    edge_nodes = np.array([[0, 1, 2, 3], [3, 7, 11, 15], [12, 13, 14, 15], [0, 4, 8, 12]])
    spread = np.zeros((16, 16), np.float32)
    for edge in range(4):
        for point in range(4):
            spread[edge_nodes[edge, point], edge * 4 + point] = 1.0
    denom = 1.0 + spread.sum(axis=1)
    quarter = np.zeros((4, 16), np.float32)
    for row_a in range(4):
        for row_b in range(4):
            quarter[row_a // 2 * 2 + row_b // 2, row_a * 4 + row_b] = 0.25
    return (laplace, spread, denom, quarter)


def matched_points(links):
    other_edge = links // 2 % 4
    reversal = links % 2
    points = jnp.arange(4, dtype=jnp.int32)
    along = jnp.where(reversal[..., None] == 1, 3 - points, points)
    base = jnp.where(other_edge == 1, 3, jnp.where(other_edge == 2, 12, 0))
    stride = jnp.where((other_edge == 1) | (other_edge == 3), 4, 1)
    return base[..., None] + stride[..., None] * along


DIRECTIONS = tuple((a, b) for a in (-1, 0, 1) for b in (-1, 0, 1) if (a, b) != (0, 0))
EDGE_NODES = ((0, 1, 2, 3), (3, 7, 11, 15), (12, 13, 14, 15), (0, 4, 8, 12))


def dyn_kernel(
    nface, ncol, row_ref, col_ref, point_ref, state_ref, out_ref, ext0, ext1, gathered, send_sem, recv_sem
):
    rows, cols, nodes, width = state_ref.shape
    face, col = lax.axis_index("face"), lax.axis_index("col")
    lanes = cols * nodes

    def device(direction):
        return (
            lax.rem(face + direction[0] + nface, nface),
            lax.rem(col + direction[1] + ncol, ncol),
        )

    barrier = pltpu.get_barrier_semaphore()
    for direction in DIRECTIONS:
        pl.semaphore_signal(
            barrier, inc=1, device_id=device(direction), device_id_type=pl.DeviceIdType.MESH
        )
    pl.semaphore_wait(barrier, len(DIRECTIONS))

    def taken(step, size):
        return {-1: 1, 0: pl.ds(1, size), 1: size}[step]

    def landed(step, size):
        return {-1: size + 1, 0: pl.ds(1, size), 1: 0}[step]

    def copy(ext, step, i):
        a, b = DIRECTIONS[i]
        return pltpu.make_async_remote_copy(
            src_ref=ext.at[taken(a, rows), taken(b, cols)],
            dst_ref=ext.at[landed(a, rows), landed(b, cols)],
            send_sem=send_sem.at[step, i],
            recv_sem=recv_sem.at[step, i],
            device_id=device(DIRECTIONS[i]),
            device_id_type=pl.DeviceIdType.MESH,
        )

    node = lax.rem(lax.broadcasted_iota(jnp.int32, (lanes, 1), 0), nodes)
    na, nb = lax.div(node, 4), lax.rem(node, 4)
    weights = [
        jnp.where(mask, KAPPA, 0.0) for mask in (na > 0, na < 3, nb > 0, nb < 3)
    ]
    own = 1.0 - (weights[0] + weights[1] + weights[2] + weights[3])
    ends = jnp.where((na == 0) | (na == 3), 1.0, 0.0) + jnp.where((nb == 0) | (nb == 3), 1.0, 0.0)
    share = 1.0 / (1.0 + ends)
    shifts = (4, lanes - 4, 1, lanes - 1)

    for r in range(rows):
        gathered[r] = jnp.zeros((cols, nodes, width), jnp.float32)

    for step in range(DSTEPS):
        src, ext = (state_ref, ext0) if step == 0 else (out_ref, ext1)
        for r in (0, rows - 1) + tuple(range(1, rows - 1)):
            flat = src[r].reshape(lanes, width)
            smooth = own * flat
            for weight, shift in zip(weights, shifts):
                smooth = smooth + weight * pltpu.roll(flat, shift, 0)
            ext[r + 1, 1 : cols + 1] = smooth.reshape(cols, nodes, width)
        copies = [copy(ext, step, i) for i in range(len(DIRECTIONS))]
        for one in copies:
            one.start()
        for one in copies:
            one.wait_recv()

        @pl.loop(0, rows * cols)
        def _(e):
            r, c = lax.div(e, cols), lax.rem(e, cols)
            terms = {}
            for k in range(4):
                for i in range(4):
                    at = e * 16 + k * 4 + i
                    value = ext[row_ref[at], col_ref[at], pl.ds(point_ref[at], 1), :]
                    terms.setdefault(EDGE_NODES[k][i], []).append(value)
            for p, values in terms.items():
                total = values[0] if len(values) == 1 else values[0] + values[1]
                gathered[r, c, p : p + 1, :] = total

        for r in range(rows):
            flat = ext[r + 1, 1 : cols + 1].reshape(lanes, width)
            fresh = (flat + gathered[r].reshape(lanes, width)) * share
            out_ref[r] = fresh.reshape(cols, nodes, width)
        for one in copies:
            one.wait_send()


def dyn_run(state, near_row, near_col, point):
    rows, cols, nodes, width = state.shape
    vmem = pl.BlockSpec(memory_space=pltpu.VMEM)
    smem = pl.BlockSpec(memory_space=pltpu.SMEM)
    halo = pltpu.VMEM((rows + 2, cols + 2, nodes, width), jnp.float32)
    return pl.pallas_call(
        functools.partial(dyn_kernel, lax.axis_size("face"), lax.axis_size("col")),
        out_shape=jax.ShapeDtypeStruct(state.shape, jnp.float32),
        in_specs=[smem, smem, smem, vmem],
        out_specs=vmem,
        scratch_shapes=[
            halo,
            halo,
            pltpu.VMEM(state.shape, jnp.float32),
            pltpu.SemaphoreType.DMA((DSTEPS, len(DIRECTIONS))),
            pltpu.SemaphoreType.DMA((DSTEPS, len(DIRECTIONS))),
        ],
        compiler_params=pltpu.CompilerParams(
            collective_id=0, has_side_effects=True, vmem_limit_bytes=32 * 2**20
        ),
    )(near_row, near_col, point, state)


def crm_kernel(force_ref, active_ref, state_hbm, out_hbm, tend_ref, held, first, final, begin, in_sem, out_sem):
    nfld, clev, cx, cols = held.shape
    part = clev // 4

    def fetch(i):
        return pltpu.make_async_copy(
            state_hbm.at[:, pl.ds(i * part, part)], held.at[:, pl.ds(i * part, part)], in_sem.at[i]
        )

    def emit(i):
        return pltpu.make_async_copy(
            final.at[:, pl.ds(i * part, part)], out_hbm.at[:, pl.ds(i * part, part)], out_sem.at[i]
        )

    for i in range(4):
        fetch(i).start()
    live = jnp.broadcast_to(active_ref[...] == 1, (cx, cols))

    def advance(src, z, store):
        above = jnp.minimum(z + 1, clev - 1)
        below = jnp.maximum(z - 1, 0)
        wind = ADVECT * src[0, z].astype(jnp.float32)
        from_east = DIFF_X - wind
        from_west = DIFF_X + wind

        def one(f):
            q = src[f, z].astype(jnp.float32)
            mean = jnp.sum(q, axis=0, keepdims=True) * (1.0 / cx)
            push = RELAX * (force_ref[f, pl.ds(z, 1), :] - mean)
            near = src[f, above].astype(jnp.float32) + src[f, below].astype(jnp.float32)
            fresh = (
                (1.0 - 2.0 * DIFF_X - 2.0 * DIFF_Z) * q
                + from_east * pltpu.roll(q, cx - 1, 0)
                + from_west * pltpu.roll(q, 1, 0)
                + DIFF_Z * near
                + push
            )
            return q, fresh, mean

        for f in range(nfld):
            q, fresh, mean = one(f)
            if f == 2:
                second = fresh
            if f == 3:
                cond = CONVERT * jnp.maximum(fresh - second, 0.0)
                fresh = fresh - cond
            if f == 4:
                fresh = fresh + cond
            store(f, z, jnp.where(live, fresh, q), mean)

    def store_first(f, z, value, mean):
        first[f, z] = value
        begin[f, pl.ds(z, 1), :] = mean

    def store_final(f, z, value, mean):
        final[f, z] = value.astype(final.dtype)
        end = jnp.sum(value, axis=0, keepdims=True) * (1.0 / cx)
        tend_ref[f, pl.ds(z, 1), :] = (end - begin[f, pl.ds(z, 1), :]) * (1.0 / CSTEPS)

    fetch(0).wait()
    fetch(1).wait()
    advance(held, 0, store_first)
    for i in range(4):
        if 1 <= i < 3:
            fetch(i + 1).wait()

        @pl.loop(max(1, i * part), (i + 1) * part)
        def _(z):
            advance(held, z, store_first)
            advance(first, z - 1, store_final)

        if i >= 1:
            emit(i - 1).start()
    advance(first, clev - 1, store_final)
    emit(3).start()
    for i in range(4):
        emit(i).wait()


def crm_run(state, forcing, active):
    nfld, clev, cx, cols = state.shape
    vmem = pl.BlockSpec(memory_space=pltpu.VMEM)
    hbm = pl.BlockSpec(memory_space=pl.ANY)
    return pl.pallas_call(
        crm_kernel,
        out_shape=(
            jax.ShapeDtypeStruct(state.shape, state.dtype),
            jax.ShapeDtypeStruct((nfld, clev, cols), jnp.float32),
        ),
        in_specs=[vmem, vmem, hbm],
        out_specs=(hbm, vmem),
        scratch_shapes=[
            pltpu.VMEM(state.shape, state.dtype),
            pltpu.VMEM(state.shape, jnp.float32),
            pltpu.VMEM(state.shape, state.dtype),
            pltpu.VMEM((nfld, clev, cols), jnp.float32),
            pltpu.SemaphoreType.DMA((4,)),
            pltpu.SemaphoreType.DMA((4,)),
        ],
        compiler_params=pltpu.CompilerParams(vmem_limit_bytes=36 * 2**20),
    )(forcing, active.reshape(1, cols), state)


def per_device(dyn_state, edge_links, phys_slot, crm_active, crm_state):
    exact = lax.Precision.HIGHEST
    laplace, spread, denom, quarter = [jnp.asarray(table) for table in node_tables()]
    rows_dev, cols_dev, nodes, width = dyn_state.shape
    nface = lax.axis_size("face")
    ncol = lax.axis_size("col")
    ndev = nface * ncol
    total_rows = rows_dev * nface
    total_cols = cols_dev * ncol
    neighbour = edge_links // 8
    pick = matched_points(edge_links)
    near_row = neighbour // total_cols
    near_col = neighbour % total_cols
    local_row = lax.broadcasted_iota(jnp.int32, (rows_dev, cols_dev, 4), 0)
    local_col = lax.broadcasted_iota(jnp.int32, (rows_dev, cols_dev, 4), 1)
    drow = (near_row - (lax.axis_index("face") * rows_dev + local_row) + 1) % total_rows - 1
    dcol = (near_col - (lax.axis_index("col") * cols_dev + local_col) + 1) % total_cols - 1
    shape = pick.shape
    state = dyn_run(
        dyn_state,
        jnp.broadcast_to((local_row + drow + 1)[..., None], shape).reshape(-1),
        jnp.broadcast_to((local_col + dcol + 1)[..., None], shape).reshape(-1),
        pick.reshape(-1),
    )
    columns = jnp.einsum("qn,rcnw->rcqw", quarter, state, precision=exact).reshape(-1, width)
    per_dev = columns.shape[0]
    count = per_dev // ndev
    depth = NFLD * CLEV
    wanted = (np.arange(NFLD)[:, None] * LEV + np.arange(CLEV)).reshape(-1)
    keep = jnp.asarray(np.arange(width)[:, None] == wanted[None, :], jnp.float32)
    keys_local = phys_slot.reshape(-1)
    rank = jnp.sum((keys_local[None, :] < keys_local[:, None]).astype(jnp.int32), axis=1)
    sorting = rank[None, :] == jnp.arange(per_dev, dtype=jnp.int32)[:, None]
    out_keys = jnp.sum(jnp.where(sorting, keys_local[None, :], 0), axis=1)
    sorting = sorting.astype(jnp.float32)
    outgoing = jnp.dot(sorting, jnp.dot(columns, keep, precision=exact), precision=exact)
    outgoing = jnp.concatenate([outgoing, out_keys[:, None].astype(jnp.float32)], axis=1)
    arrived = lax.all_to_all(
        outgoing.reshape(ndev, count, depth + 1),
        ("face", "col"),
        split_axis=0,
        concat_axis=0,
        tiled=True,
    ).reshape(per_dev, depth + 1)
    slots = arrived[:, depth].astype(jnp.int32) % per_dev
    landing = (slots[:, None] == jnp.arange(per_dev, dtype=jnp.int32)[None, :]).astype(jnp.float32)
    forcing = jnp.einsum("sw,sc->wc", arrived[:, :depth], landing, precision=exact)
    crm_new, tend = crm_run(crm_state, forcing.reshape(NFLD, CLEV, per_dev), crm_active)
    tend_rows = jnp.einsum("sc,wc->sw", landing, tend.reshape(depth, per_dev), precision=exact)
    returned = lax.all_to_all(
        tend_rows.reshape(ndev, count, depth),
        ("face", "col"),
        split_axis=0,
        concat_axis=0,
        tiled=True,
    )
    placed = jnp.einsum("pi,pw->iw", sorting, returned.reshape(per_dev, depth), precision=exact)
    column_tend = placed.reshape(rows_dev, cols_dev, 4, depth)
    return (state, column_tend, crm_new)


def solution(mesh):
    return jax.shard_map(
        per_device,
        mesh=mesh,
        in_specs=(
            P("face", "col", None, None),
            P("face", "col", None),
            P("face", "col", None),
            P(("face", "col")),
            P(None, None, None, ("face", "col")),
        ),
        out_specs=(
            P("face", "col", None, None),
            P("face", "col", None, None),
            P(None, None, None, ("face", "col")),
        ),
        check_vma=False,
    )
```

```python
import functools

import jax
import jax.numpy as jnp
import numpy as np
from jax import lax
from jax.experimental import pallas as pl
from jax.experimental.pallas import tpu as pltpu
from jax.sharding import PartitionSpec as P

NFLD = 10
LEV = 72
CLEV = 32
DSTEPS = 2
CSTEPS = 2


KAPPA = 0.1
ADVECT = 0.1
DIFF_X = 0.2
DIFF_Z = 0.1
RELAX = 0.2
CONVERT = 0.5


def node_tables():
    laplace = np.zeros((16, 16), np.float32)
    for row_a in range(4):
        for row_b in range(4):
            here = row_a * 4 + row_b
            for step_a, step_b in ((1, 0), (-1, 0), (0, 1), (0, -1)):
                near_a, near_b = (row_a + step_a, row_b + step_b)
                if 0 <= near_a < 4 and 0 <= near_b < 4:
                    laplace[here, near_a * 4 + near_b] += 1.0
                    laplace[here, here] -= 1.0
    edge_nodes = np.array([[0, 1, 2, 3], [3, 7, 11, 15], [12, 13, 14, 15], [0, 4, 8, 12]])
    spread = np.zeros((16, 16), np.float32)
    for edge in range(4):
        for point in range(4):
            spread[edge_nodes[edge, point], edge * 4 + point] = 1.0
    denom = 1.0 + spread.sum(axis=1)
    quarter = np.zeros((4, 16), np.float32)
    for row_a in range(4):
        for row_b in range(4):
            quarter[row_a // 2 * 2 + row_b // 2, row_a * 4 + row_b] = 0.25
    return (laplace, spread, denom, quarter)


def matched_points(links):
    other_edge = links // 2 % 4
    reversal = links % 2
    points = jnp.arange(4, dtype=jnp.int32)
    along = jnp.where(reversal[..., None] == 1, 3 - points, points)
    base = jnp.where(other_edge == 1, 3, jnp.where(other_edge == 2, 12, 0))
    stride = jnp.where((other_edge == 1) | (other_edge == 3), 4, 1)
    point = base[..., None] + stride[..., None] * along
    skipped = sum(jnp.where(point > inner, 1, 0) for inner in (5, 6, 9, 10))
    return point - skipped


SIDES = ((-1, 0), (1, 0), (0, -1), (0, 1))
EDGE_NODES = ((0, 1, 2, 3), (3, 7, 11, 15), (12, 13, 14, 15), (0, 4, 8, 12))
RIM = (0, 1, 2, 3, 4, 7, 8, 11, 12, 13, 14, 15)
SIDE = 16
RUNS = ((0, 0, 5), (5, 7, 2), (7, 11, 5))


def dyn_kernel(
    nface, ncol, row_ref, point_ref, state_ref, out_ref, ext0, ext1, smoothed, gathered, send_sem, recv_sem
):
    rows, cols, nodes, width = state_ref.shape
    face, col = lax.axis_index("face"), lax.axis_index("col")
    lanes = cols * nodes
    rim = len(RIM)
    own_cols = pl.ds(SIDE, cols * rim)
    first_col, last_col = pl.ds(SIDE, SIDE), pl.ds(cols * rim, SIDE)
    west_halo, east_halo = pl.ds(0, SIDE), pl.ds(SIDE + cols * rim, SIDE)
    own_rows = pl.ds(1, rows)

    def device(side):
        return (
            lax.rem(face + side[0] + nface, nface),
            lax.rem(col + side[1] + ncol, ncol),
        )

    barrier = pltpu.get_barrier_semaphore()
    for side in SIDES:
        pl.semaphore_signal(
            barrier, inc=1, device_id=device(side), device_id_type=pl.DeviceIdType.MESH
        )
    pl.semaphore_wait(barrier, len(SIDES))

    plan = (
        ((1, own_cols), (rows + 1, own_cols), SIDES[0]),
        ((rows, own_cols), (0, own_cols), SIDES[1]),
        ((own_rows, first_col), (own_rows, east_halo), SIDES[2]),
        ((own_rows, last_col), (own_rows, west_halo), SIDES[3]),
        ((rows + 1, first_col), (rows + 1, east_halo), SIDES[2]),
        ((rows + 1, last_col), (rows + 1, west_halo), SIDES[3]),
        ((0, first_col), (0, east_halo), SIDES[2]),
        ((0, last_col), (0, west_halo), SIDES[3]),
    )

    def copy(ext, step, i):
        here, there, side = plan[i]
        return pltpu.make_async_remote_copy(
            src_ref=ext.at[here],
            dst_ref=ext.at[there],
            send_sem=send_sem.at[step, i],
            recv_sem=recv_sem.at[step, i],
            device_id=device(side),
            device_id_type=pl.DeviceIdType.MESH,
        )

    node = lax.rem(lax.broadcasted_iota(jnp.int32, (lanes, 1), 0), nodes)
    na, nb = lax.div(node, 4), lax.rem(node, 4)
    weights = [jnp.where(mask, KAPPA, 0.0) for mask in (na > 0, na < 3, nb > 0, nb < 3)]
    own = 1.0 - (weights[0] + weights[1] + weights[2] + weights[3])
    ends = jnp.where((na == 0) | (na == 3), 1.0, 0.0) + jnp.where((nb == 0) | (nb == 3), 1.0, 0.0)
    share = 1.0 / (1.0 + ends)
    shifts = (4, lanes - 4, 1, lanes - 1)

    for r in range(rows):
        gathered[r] = jnp.zeros((cols, nodes, width), jnp.float32)

    for step in range(DSTEPS):
        src, ext = (state_ref, ext0) if step == 0 else (out_ref, ext1)
        copies = [copy(ext, step, i) for i in range(len(plan))]
        for r in (0, rows - 1) + tuple(range(1, rows - 1)):
            flat = src[r].reshape(lanes, width)
            smooth = own * flat
            for weight, shift in zip(weights, shifts):
                smooth = smooth + weight * pltpu.roll(flat, shift, 0)
            smoothed[r] = smooth.reshape(cols, nodes, width)
            for c in range(cols):
                for to, at, size in RUNS:
                    ext[r + 1, pl.ds(SIDE + c * rim + to, size), :] = smoothed[r, c, pl.ds(at, size), :]
            if r == 0:
                copies[0].start()
            if r == rows - 1:
                copies[1].start()
        copies[2].start()
        copies[3].start()
        copies[0].wait_recv()
        copies[4].start()
        copies[5].start()
        copies[1].wait_recv()
        for one in copies[6:]:
            one.start()
        for one in copies[2:]:
            one.wait_recv()

        @pl.loop(0, rows * cols)
        def _(e):
            r, c = lax.div(e, cols), lax.rem(e, cols)
            terms = {}
            for k in range(4):
                for i in range(4):
                    at = e * 16 + k * 4 + i
                    value = ext[row_ref[at], pl.ds(point_ref[at], 1), :]
                    terms.setdefault(EDGE_NODES[k][i], []).append(value)
            for p, values in terms.items():
                total = values[0] if len(values) == 1 else values[0] + values[1]
                gathered[r, c, p : p + 1, :] = total

        for r in range(rows):
            out_ref[r] = (
                (smoothed[r].reshape(lanes, width) + gathered[r].reshape(lanes, width)) * share
            ).reshape(cols, nodes, width)
        for one in copies:
            one.wait_send()


def dyn_run(state, near_row, point):
    rows, cols, nodes, width = state.shape
    vmem = pl.BlockSpec(memory_space=pltpu.VMEM)
    smem = pl.BlockSpec(memory_space=pltpu.SMEM)
    halo = pltpu.VMEM((rows + 2, cols * len(RIM) + 2 * SIDE, width), jnp.float32)
    return pl.pallas_call(
        functools.partial(dyn_kernel, lax.axis_size("face"), lax.axis_size("col")),
        out_shape=jax.ShapeDtypeStruct(state.shape, jnp.float32),
        in_specs=[smem, smem, vmem],
        out_specs=vmem,
        scratch_shapes=[
            halo,
            halo,
            pltpu.VMEM(state.shape, jnp.float32),
            pltpu.VMEM(state.shape, jnp.float32),
            pltpu.SemaphoreType.DMA((DSTEPS, 8)),
            pltpu.SemaphoreType.DMA((DSTEPS, 8)),
        ],
        compiler_params=pltpu.CompilerParams(
            collective_id=0, has_side_effects=True, vmem_limit_bytes=32 * 2**20
        ),
    )(near_row, point, state)


def crm_kernel(force_ref, active_ref, state_hbm, out_hbm, tend_ref, held, first, final, begin, in_sem, out_sem):
    nfld, clev, cx, cols = held.shape
    part = clev // 4

    def fetch(i):
        return pltpu.make_async_copy(
            state_hbm.at[:, pl.ds(i * part, part)], held.at[:, pl.ds(i * part, part)], in_sem.at[i]
        )

    def emit(i):
        return pltpu.make_async_copy(
            final.at[:, pl.ds(i * part, part)], out_hbm.at[:, pl.ds(i * part, part)], out_sem.at[i]
        )

    for i in range(4):
        fetch(i).start()
    live = jnp.broadcast_to(active_ref[...] == 1, (cx, cols))

    def advance(src, z, store):
        above = jnp.minimum(z + 1, clev - 1)
        below = jnp.maximum(z - 1, 0)
        wind = ADVECT * src[0, z].astype(jnp.float32)
        from_east = DIFF_X - wind
        from_west = DIFF_X + wind

        def one(f):
            q = src[f, z].astype(jnp.float32)
            mean = jnp.sum(q, axis=0, keepdims=True) * (1.0 / cx)
            push = RELAX * (force_ref[f, pl.ds(z, 1), :] - mean)
            near = src[f, above].astype(jnp.float32) + src[f, below].astype(jnp.float32)
            fresh = (
                (1.0 - 2.0 * DIFF_X - 2.0 * DIFF_Z) * q
                + from_east * pltpu.roll(q, cx - 1, 0)
                + from_west * pltpu.roll(q, 1, 0)
                + DIFF_Z * near
                + push
            )
            return q, fresh, mean

        for f in range(nfld):
            q, fresh, mean = one(f)
            if f == 2:
                second = fresh
            if f == 3:
                cond = CONVERT * jnp.maximum(fresh - second, 0.0)
                fresh = fresh - cond
            if f == 4:
                fresh = fresh + cond
            store(f, z, jnp.where(live, fresh, q), mean)

    def store_first(f, z, value, mean):
        first[f, z] = value
        begin[f, pl.ds(z, 1), :] = mean

    def store_final(f, z, value, mean):
        final[f, z] = value.astype(final.dtype)
        end = jnp.sum(value, axis=0, keepdims=True) * (1.0 / cx)
        tend_ref[f, pl.ds(z, 1), :] = (end - begin[f, pl.ds(z, 1), :]) * (1.0 / CSTEPS)

    fetch(0).wait()
    fetch(1).wait()
    advance(held, 0, store_first)
    for i in range(4):
        if 1 <= i < 3:
            fetch(i + 1).wait()

        @pl.loop(max(1, i * part), (i + 1) * part)
        def _(z):
            advance(held, z, store_first)
            advance(first, z - 1, store_final)

        if i >= 1:
            emit(i - 1).start()
    advance(first, clev - 1, store_final)
    emit(3).start()
    for i in range(4):
        emit(i).wait()


def crm_run(state, forcing, active):
    nfld, clev, cx, cols = state.shape
    vmem = pl.BlockSpec(memory_space=pltpu.VMEM)
    hbm = pl.BlockSpec(memory_space=pl.ANY)
    return pl.pallas_call(
        crm_kernel,
        out_shape=(
            jax.ShapeDtypeStruct(state.shape, state.dtype),
            jax.ShapeDtypeStruct((nfld, clev, cols), jnp.float32),
        ),
        in_specs=[vmem, vmem, hbm],
        out_specs=(hbm, vmem),
        scratch_shapes=[
            pltpu.VMEM(state.shape, state.dtype),
            pltpu.VMEM(state.shape, jnp.float32),
            pltpu.VMEM(state.shape, state.dtype),
            pltpu.VMEM((nfld, clev, cols), jnp.float32),
            pltpu.SemaphoreType.DMA((4,)),
            pltpu.SemaphoreType.DMA((4,)),
        ],
        compiler_params=pltpu.CompilerParams(vmem_limit_bytes=60 * 2**20),
    )(forcing, active.reshape(1, cols), state)


def per_device(dyn_state, edge_links, phys_slot, crm_active, crm_state):
    exact = lax.Precision.HIGHEST
    laplace, spread, denom, quarter = [jnp.asarray(table) for table in node_tables()]
    rows_dev, cols_dev, nodes, width = dyn_state.shape
    nface = lax.axis_size("face")
    ncol = lax.axis_size("col")
    ndev = nface * ncol
    total_rows = rows_dev * nface
    total_cols = cols_dev * ncol
    neighbour = edge_links // 8
    pick = matched_points(edge_links)
    near_row = neighbour // total_cols
    near_col = neighbour % total_cols
    local_row = lax.broadcasted_iota(jnp.int32, (rows_dev, cols_dev, 4), 0)
    local_col = lax.broadcasted_iota(jnp.int32, (rows_dev, cols_dev, 4), 1)
    drow = (near_row - (lax.axis_index("face") * rows_dev + local_row) + 1) % total_rows - 1
    dcol = (near_col - (lax.axis_index("col") * cols_dev + local_col) + 1) % total_cols - 1
    shape = pick.shape
    state = dyn_run(
        dyn_state,
        jnp.broadcast_to((local_row + drow + 1)[..., None], shape).reshape(-1),
        ((local_col + dcol)[..., None] * len(RIM) + SIDE + pick).reshape(-1),
    )
    columns = jnp.einsum("qn,rcnw->rcqw", quarter, state, precision=exact).reshape(-1, width)
    per_dev = columns.shape[0]
    count = per_dev // ndev
    depth = NFLD * CLEV
    wanted = (np.arange(NFLD)[:, None] * LEV + np.arange(CLEV)).reshape(-1)
    keep = jnp.asarray(np.arange(width)[:, None] == wanted[None, :], jnp.float32)
    keys_local = phys_slot.reshape(-1)
    rank = jnp.sum((keys_local[None, :] < keys_local[:, None]).astype(jnp.int32), axis=1)
    sorting = rank[None, :] == jnp.arange(per_dev, dtype=jnp.int32)[:, None]
    out_keys = jnp.sum(jnp.where(sorting, keys_local[None, :], 0), axis=1)
    sorting = sorting.astype(jnp.float32)
    outgoing = jnp.dot(sorting, jnp.dot(columns, keep, precision=exact), precision=exact)
    outgoing = jnp.concatenate([outgoing, out_keys[:, None].astype(jnp.float32)], axis=1)
    arrived = lax.all_to_all(
        outgoing.reshape(ndev, count, depth + 1),
        ("face", "col"),
        split_axis=0,
        concat_axis=0,
        tiled=True,
    ).reshape(per_dev, depth + 1)
    slots = arrived[:, depth].astype(jnp.int32) % per_dev
    landing = (slots[:, None] == jnp.arange(per_dev, dtype=jnp.int32)[None, :]).astype(jnp.float32)
    forcing = jnp.einsum("sw,sc->wc", arrived[:, :depth], landing, precision=exact)
    crm_new, tend = crm_run(crm_state, forcing.reshape(NFLD, CLEV, per_dev), crm_active)
    tend_rows = jnp.einsum("sc,wc->sw", landing, tend.reshape(depth, per_dev), precision=exact)
    returned = lax.all_to_all(
        tend_rows.reshape(ndev, count, depth),
        ("face", "col"),
        split_axis=0,
        concat_axis=0,
        tiled=True,
    )
    placed = jnp.einsum("pi,pw->iw", sorting, returned.reshape(per_dev, depth), precision=exact)
    column_tend = placed.reshape(rows_dev, cols_dev, 4, depth)
    return (state, column_tend, crm_new)


def solution(mesh):
    return jax.shard_map(
        per_device,
        mesh=mesh,
        in_specs=(
            P("face", "col", None, None),
            P("face", "col", None),
            P("face", "col", None),
            P(("face", "col")),
            P(None, None, None, ("face", "col")),
        ),
        out_specs=(
            P("face", "col", None, None),
            P("face", "col", None, None),
            P(None, None, None, ("face", "col")),
        ),
        check_vma=False,
    )
```

```python
import functools

import jax
import jax.numpy as jnp
import numpy as np
from jax import lax
from jax.experimental import pallas as pl
from jax.experimental.pallas import tpu as pltpu
from jax.sharding import PartitionSpec as P

NFLD = 10
LEV = 72
CLEV = 32
DSTEPS = 2
CSTEPS = 2


KAPPA = 0.1
ADVECT = 0.1
DIFF_X = 0.2
DIFF_Z = 0.1
RELAX = 0.2
CONVERT = 0.5


def node_tables():
    laplace = np.zeros((16, 16), np.float32)
    for row_a in range(4):
        for row_b in range(4):
            here = row_a * 4 + row_b
            for step_a, step_b in ((1, 0), (-1, 0), (0, 1), (0, -1)):
                near_a, near_b = (row_a + step_a, row_b + step_b)
                if 0 <= near_a < 4 and 0 <= near_b < 4:
                    laplace[here, near_a * 4 + near_b] += 1.0
                    laplace[here, here] -= 1.0
    edge_nodes = np.array([[0, 1, 2, 3], [3, 7, 11, 15], [12, 13, 14, 15], [0, 4, 8, 12]])
    spread = np.zeros((16, 16), np.float32)
    for edge in range(4):
        for point in range(4):
            spread[edge_nodes[edge, point], edge * 4 + point] = 1.0
    denom = 1.0 + spread.sum(axis=1)
    quarter = np.zeros((4, 16), np.float32)
    for row_a in range(4):
        for row_b in range(4):
            quarter[row_a // 2 * 2 + row_b // 2, row_a * 4 + row_b] = 0.25
    return (laplace, spread, denom, quarter)


def matched_points(links):
    other_edge = links // 2 % 4
    reversal = links % 2
    points = jnp.arange(4, dtype=jnp.int32)
    along = jnp.where(reversal[..., None] == 1, 3 - points, points)
    base = jnp.where(other_edge == 1, 3, jnp.where(other_edge == 2, 12, 0))
    stride = jnp.where((other_edge == 1) | (other_edge == 3), 4, 1)
    point = base[..., None] + stride[..., None] * along
    skipped = sum(jnp.where(point > inner, 1, 0) for inner in (5, 6, 9, 10))
    return point - skipped


SIDES = ((-1, 0), (1, 0), (0, -1), (0, 1))
EDGE_NODES = ((0, 1, 2, 3), (3, 7, 11, 15), (12, 13, 14, 15), (0, 4, 8, 12))
RIM = (0, 1, 2, 3, 4, 7, 8, 11, 12, 13, 14, 15)
SIDE = 16
RUNS = ((0, 0, 5), (5, 7, 2), (7, 11, 5))


def dyn_kernel(
    nface, ncol, row_ref, point_ref, state_ref, out_ref, ext0, ext1, smoothed, gathered, send_sem, recv_sem
):
    rows, cols, nodes, width = state_ref.shape
    face, col = lax.axis_index("face"), lax.axis_index("col")
    lanes = cols * nodes
    rim = len(RIM)
    own_cols = pl.ds(SIDE, cols * rim)
    first_col, last_col = pl.ds(SIDE, SIDE), pl.ds(cols * rim, SIDE)
    west_halo, east_halo = pl.ds(0, SIDE), pl.ds(SIDE + cols * rim, SIDE)
    own_rows = pl.ds(1, rows)

    def device(side):
        return (
            lax.rem(face + side[0] + nface, nface),
            lax.rem(col + side[1] + ncol, ncol),
        )

    barrier = pltpu.get_barrier_semaphore()
    for side in SIDES:
        pl.semaphore_signal(
            barrier, inc=1, device_id=device(side), device_id_type=pl.DeviceIdType.MESH
        )
    pl.semaphore_wait(barrier, len(SIDES))

    plan = (
        ((1, own_cols), (rows + 1, own_cols), SIDES[0]),
        ((rows, own_cols), (0, own_cols), SIDES[1]),
        ((own_rows, first_col), (own_rows, east_halo), SIDES[2]),
        ((own_rows, last_col), (own_rows, west_halo), SIDES[3]),
        ((rows + 1, first_col), (rows + 1, east_halo), SIDES[2]),
        ((rows + 1, last_col), (rows + 1, west_halo), SIDES[3]),
        ((0, first_col), (0, east_halo), SIDES[2]),
        ((0, last_col), (0, west_halo), SIDES[3]),
    )

    def copy(ext, step, i):
        here, there, side = plan[i]
        return pltpu.make_async_remote_copy(
            src_ref=ext.at[here],
            dst_ref=ext.at[there],
            send_sem=send_sem.at[step, i],
            recv_sem=recv_sem.at[step, i],
            device_id=device(side),
            device_id_type=pl.DeviceIdType.MESH,
        )

    node = lax.rem(lax.broadcasted_iota(jnp.int32, (lanes, 1), 0), nodes)
    na, nb = lax.div(node, 4), lax.rem(node, 4)
    weights = [jnp.where(mask, KAPPA, 0.0) for mask in (na > 0, na < 3, nb > 0, nb < 3)]
    own = 1.0 - (weights[0] + weights[1] + weights[2] + weights[3])
    ends = jnp.where((na == 0) | (na == 3), 1.0, 0.0) + jnp.where((nb == 0) | (nb == 3), 1.0, 0.0)
    share = 1.0 / (1.0 + ends)
    shifts = (4, lanes - 4, 1, lanes - 1)

    for r in range(rows):
        gathered[r] = jnp.zeros((cols, nodes, width), jnp.float32)

    for step in range(DSTEPS):
        src, ext = (state_ref, ext0) if step == 0 else (out_ref, ext1)
        copies = [copy(ext, step, i) for i in range(len(plan))]
        for r in (0, rows - 1) + tuple(range(1, rows - 1)):
            flat = src[r].reshape(lanes, width)
            smooth = own * flat
            for weight, shift in zip(weights, shifts):
                smooth = smooth + weight * pltpu.roll(flat, shift, 0)
            smoothed[r] = smooth.reshape(cols, nodes, width)
            for c in range(cols):
                for to, at, size in RUNS:
                    ext[r + 1, pl.ds(SIDE + c * rim + to, size), :] = smoothed[r, c, pl.ds(at, size), :]
            if r == 0:
                copies[0].start()
            if r == rows - 1:
                copies[1].start()
        copies[2].start()
        copies[3].start()
        copies[0].wait_recv()
        copies[4].start()
        copies[5].start()
        copies[1].wait_recv()
        for one in copies[6:]:
            one.start()
        for one in copies[2:]:
            one.wait_recv()

        @pl.loop(0, rows * cols)
        def _(e):
            r, c = lax.div(e, cols), lax.rem(e, cols)
            terms = {}
            for k in range(4):
                for i in range(4):
                    at = e * 16 + k * 4 + i
                    value = ext[row_ref[at], pl.ds(point_ref[at], 1), :]
                    terms.setdefault(EDGE_NODES[k][i], []).append(value)
            for p, values in terms.items():
                total = values[0] if len(values) == 1 else values[0] + values[1]
                gathered[r, c, p : p + 1, :] = total

        for r in range(rows):
            out_ref[r] = (
                (smoothed[r].reshape(lanes, width) + gathered[r].reshape(lanes, width)) * share
            ).reshape(cols, nodes, width)
        for one in copies:
            one.wait_send()


def dyn_run(state, near_row, point):
    rows, cols, nodes, width = state.shape
    vmem = pl.BlockSpec(memory_space=pltpu.VMEM)
    smem = pl.BlockSpec(memory_space=pltpu.SMEM)
    halo = pltpu.VMEM((rows + 2, cols * len(RIM) + 2 * SIDE, width), jnp.float32)
    return pl.pallas_call(
        functools.partial(dyn_kernel, lax.axis_size("face"), lax.axis_size("col")),
        out_shape=jax.ShapeDtypeStruct(state.shape, jnp.float32),
        in_specs=[smem, smem, vmem],
        out_specs=vmem,
        scratch_shapes=[
            halo,
            halo,
            pltpu.VMEM(state.shape, jnp.float32),
            pltpu.VMEM(state.shape, jnp.float32),
            pltpu.SemaphoreType.DMA((DSTEPS, 8)),
            pltpu.SemaphoreType.DMA((DSTEPS, 8)),
        ],
        compiler_params=pltpu.CompilerParams(
            collective_id=0, has_side_effects=True, vmem_limit_bytes=32 * 2**20
        ),
    )(near_row, point, state)


def crm_kernel(force_ref, active_ref, state_hbm, out_hbm, tend_ref, held, first, final, begin, in_sem, out_sem):
    nfld, clev, cx, cols = held.shape
    part = clev // 8

    def fetch(i):
        return pltpu.make_async_copy(
            state_hbm.at[:, pl.ds(i * part, part)], held.at[:, pl.ds(i * part, part)], in_sem.at[i]
        )

    def emit(i):
        return pltpu.make_async_copy(
            final.at[:, pl.ds(i * part, part)], out_hbm.at[:, pl.ds(i * part, part)], out_sem.at[i]
        )

    for i in range(8):
        fetch(i).start()
    live = jnp.broadcast_to(active_ref[...] == 1, (cx, cols))

    def advance(src, z, store):
        above = jnp.minimum(z + 1, clev - 1)
        below = jnp.maximum(z - 1, 0)
        wind = ADVECT * src[0, z].astype(jnp.float32)
        from_east = DIFF_X - wind
        from_west = DIFF_X + wind

        def one(f):
            q = src[f, z].astype(jnp.float32)
            mean = jnp.sum(q, axis=0, keepdims=True) * (1.0 / cx)
            push = RELAX * (force_ref[f, pl.ds(z, 1), :] - mean)
            near = src[f, above].astype(jnp.float32) + src[f, below].astype(jnp.float32)
            fresh = (
                (1.0 - 2.0 * DIFF_X - 2.0 * DIFF_Z) * q
                + from_east * pltpu.roll(q, cx - 1, 0)
                + from_west * pltpu.roll(q, 1, 0)
                + DIFF_Z * near
                + push
            )
            return q, fresh, mean

        for f in range(nfld):
            q, fresh, mean = one(f)
            if f == 2:
                second = fresh
            if f == 3:
                cond = CONVERT * jnp.maximum(fresh - second, 0.0)
                fresh = fresh - cond
            if f == 4:
                fresh = fresh + cond
            store(f, z, jnp.where(live, fresh, q), mean)

    def store_first(f, z, value, mean):
        first[f, z] = value
        begin[f, pl.ds(z, 1), :] = mean

    def store_final(f, z, value, mean):
        final[f, z] = value.astype(final.dtype)
        end = jnp.sum(value, axis=0, keepdims=True) * (1.0 / cx)
        tend_ref[f, pl.ds(z, 1), :] = (end - begin[f, pl.ds(z, 1), :]) * (1.0 / CSTEPS)

    fetch(0).wait()
    fetch(1).wait()
    advance(held, 0, store_first)
    for i in range(8):
        if 1 <= i < 7:
            fetch(i + 1).wait()

        @pl.loop(max(1, i * part), (i + 1) * part)
        def _(z):
            advance(held, z, store_first)
            advance(first, z - 1, store_final)

        if i >= 1:
            emit(i - 1).start()
    advance(first, clev - 1, store_final)
    emit(7).start()
    for i in range(8):
        emit(i).wait()


def crm_run(state, forcing, active):
    nfld, clev, cx, cols = state.shape
    vmem = pl.BlockSpec(memory_space=pltpu.VMEM)
    hbm = pl.BlockSpec(memory_space=pl.ANY)
    return pl.pallas_call(
        crm_kernel,
        out_shape=(
            jax.ShapeDtypeStruct(state.shape, state.dtype),
            jax.ShapeDtypeStruct((nfld, clev, cols), jnp.float32),
        ),
        in_specs=[vmem, vmem, hbm],
        out_specs=(hbm, vmem),
        scratch_shapes=[
            pltpu.VMEM(state.shape, state.dtype),
            pltpu.VMEM(state.shape, jnp.float32),
            pltpu.VMEM(state.shape, state.dtype),
            pltpu.VMEM((nfld, clev, cols), jnp.float32),
            pltpu.SemaphoreType.DMA((8,)),
            pltpu.SemaphoreType.DMA((8,)),
        ],
        compiler_params=pltpu.CompilerParams(vmem_limit_bytes=60 * 2**20),
    )(forcing, active.reshape(1, cols), state)


def per_device(dyn_state, edge_links, phys_slot, crm_active, crm_state):
    exact = lax.Precision.HIGHEST
    laplace, spread, denom, quarter = [jnp.asarray(table) for table in node_tables()]
    rows_dev, cols_dev, nodes, width = dyn_state.shape
    nface = lax.axis_size("face")
    ncol = lax.axis_size("col")
    ndev = nface * ncol
    total_rows = rows_dev * nface
    total_cols = cols_dev * ncol
    neighbour = edge_links // 8
    pick = matched_points(edge_links)
    near_row = neighbour // total_cols
    near_col = neighbour % total_cols
    local_row = lax.broadcasted_iota(jnp.int32, (rows_dev, cols_dev, 4), 0)
    local_col = lax.broadcasted_iota(jnp.int32, (rows_dev, cols_dev, 4), 1)
    drow = (near_row - (lax.axis_index("face") * rows_dev + local_row) + 1) % total_rows - 1
    dcol = (near_col - (lax.axis_index("col") * cols_dev + local_col) + 1) % total_cols - 1
    shape = pick.shape
    state = dyn_run(
        dyn_state,
        jnp.broadcast_to((local_row + drow + 1)[..., None], shape).reshape(-1),
        ((local_col + dcol)[..., None] * len(RIM) + SIDE + pick).reshape(-1),
    )
    columns = jnp.einsum("qn,rcnw->rcqw", quarter, state, precision=exact).reshape(-1, width)
    per_dev = columns.shape[0]
    count = per_dev // ndev
    depth = NFLD * CLEV
    wanted = (np.arange(NFLD)[:, None] * LEV + np.arange(CLEV)).reshape(-1)
    keep = jnp.asarray(np.arange(width)[:, None] == wanted[None, :], jnp.float32)
    keys_local = phys_slot.reshape(-1)
    rank = jnp.sum((keys_local[None, :] < keys_local[:, None]).astype(jnp.int32), axis=1)
    sorting = rank[None, :] == jnp.arange(per_dev, dtype=jnp.int32)[:, None]
    out_keys = jnp.sum(jnp.where(sorting, keys_local[None, :], 0), axis=1)
    sorting = sorting.astype(jnp.float32)
    outgoing = jnp.dot(sorting, jnp.dot(columns, keep, precision=exact), precision=exact)
    outgoing = jnp.concatenate([outgoing, out_keys[:, None].astype(jnp.float32)], axis=1)
    arrived = lax.all_to_all(
        outgoing.reshape(ndev, count, depth + 1),
        ("face", "col"),
        split_axis=0,
        concat_axis=0,
        tiled=True,
    ).reshape(per_dev, depth + 1)
    slots = arrived[:, depth].astype(jnp.int32) % per_dev
    landing = (slots[:, None] == jnp.arange(per_dev, dtype=jnp.int32)[None, :]).astype(jnp.float32)
    forcing = jnp.einsum("sw,sc->wc", arrived[:, :depth], landing, precision=exact)
    crm_new, tend = crm_run(crm_state, forcing.reshape(NFLD, CLEV, per_dev), crm_active)
    tend_rows = jnp.einsum("sc,wc->sw", landing, tend.reshape(depth, per_dev), precision=exact)
    returned = lax.all_to_all(
        tend_rows.reshape(ndev, count, depth),
        ("face", "col"),
        split_axis=0,
        concat_axis=0,
        tiled=True,
    )
    placed = jnp.einsum("pi,pw->iw", sorting, returned.reshape(per_dev, depth), precision=exact)
    column_tend = placed.reshape(rows_dev, cols_dev, 4, depth)
    return (state, column_tend, crm_new)


def solution(mesh):
    return jax.shard_map(
        per_device,
        mesh=mesh,
        in_specs=(
            P("face", "col", None, None),
            P("face", "col", None),
            P("face", "col", None),
            P(("face", "col")),
            P(None, None, None, ("face", "col")),
        ),
        out_specs=(
            P("face", "col", None, None),
            P("face", "col", None, None),
            P(None, None, None, ("face", "col")),
        ),
        check_vma=False,
    )
```
